512 devices in a mesh: sx: 32 (over y_lo, x, core), sy: 16 (over z, y_hi).
Axes of the slice: x: 4, y: 8 (y_hi: 2, y_lo: 4; y = y_hi * 4 + y_lo), z: 8, core: 2. Of those that a mesh axis runs over, the one named last changes fastest.
Arguments:
- schur_x: float32 [64, 16, 512, 512], P('sx', 'sy'), may hold values from -1 to 5, as said below
- schur_y: float32 [32, 32, 512, 512], P('sx', 'sy'), may hold values from -1 to 5, as said below
- residual_x: float32 [64, 16, 32, 512], P('sx', 'sy'), may hold values from -36 to 36
- residual_y: float32 [32, 32, 32, 512], P('sx', 'sy'), may hold values from -36 to 36
- basis_x: float32 [64, 16, 6, 512], P('sx', 'sy'), may hold values from -0.9 to 0.9
- basis_y: float32 [32, 32, 6, 512], P('sx', 'sy'), may hold values from -0.9 to 0.9
- couple_x: float32 [32, 16, 6, 6], P('sx', 'sy'), may hold values from -0.3 to 0.1
- couple_y: float32 [32, 16, 6, 6], P('sx', 'sy'), may hold values from -0.3 to 0.1
- coarse_shift: float32 [32, 16, 6], P('sx', 'sy'), may hold values from 0.05 to 0.5
Outputs:
- average_x: float32 [64, 16, 32, 512], P('sx', 'sy')
- average_y: float32 [32, 32, 32, 512], P('sx', 'sy')
- coarse_values: float32 [32, 16, 6, 32], P('sx', 'sy')
The draws below stay inside these ranges and needn't reach their ends.
Inputs may be any that keep to these rules, and one draw needn't show every extreme that they name: `schur_x`: every block is symmetric positive definite. `schur_y`: every block is symmetric positive definite.
All inputs are finite; a program needn't handle non-finite values.
Results may differ from the reference program's by a relative error of at most 0.0003.
Values sent between devices are 32-bit elements; how exact they have to be, the bound alone decides.
A program may use at most 128 MiB of HBM per device.

```python
import math
import jax
import jax.numpy as jnp
from jax import lax

F = 512
R = 32
PC = 6
CITERS = 8
SUBX = 32
SUBY = 16


def make_blocks(key, count):
    keys = jax.random.split(key, count)

    def single(subkey):
        first_key, second_key, third_key = jax.random.split(subkey, 3)
        factor = jnp.clip(jax.random.normal(first_key, (F, F), jnp.float32), -4.0, 4.0)
        spread = jnp.exp(jax.random.uniform(second_key, (F,), jnp.float32, math.log(0.003), math.log(0.03)))
        weights = jnp.exp(jax.random.uniform(third_key, (F,), jnp.float32, math.log(0.001), math.log(2.0)))
        product = jnp.dot(factor * weights[None, :], factor.T, precision=lax.Precision.HIGHEST)
        return product / F + jnp.diag(spread)
    return lax.map(single, keys)


def make_residual(key, rows, cols, position):
    first_key, second_key = jax.random.split(key, 2)
    base = jnp.clip(jax.random.normal(first_key, (rows, cols, R, F), jnp.float32), -6.0, 6.0)
    device_scale = jnp.exp(jax.random.uniform(second_key, (rows, cols, 1, 1), jnp.float32, 0.0, math.log(2.0)))
    growth = jnp.exp(position * math.log(3.0))
    return base * device_scale * growth


def draw_schur_x(key, part):
    return make_blocks(key, 2 * SUBX * SUBY).reshape(2 * SUBX, SUBY, F, F)


def draw_schur_y(key, part):
    return make_blocks(key, 2 * SUBX * SUBY).reshape(SUBX, 2 * SUBY, F, F)


def draw_residual_x(key, part):
    position = (jnp.arange(2 * SUBX) // 2).astype(jnp.float32) / (SUBX - 1)
    return make_residual(key, 2 * SUBX, SUBY, position[:, None, None, None])


def draw_residual_y(key, part):
    position = jnp.arange(SUBX).astype(jnp.float32) / (SUBX - 1)
    return make_residual(key, SUBX, 2 * SUBY, position[:, None, None, None])


def levels(own_key, extent, shards, least, high):
    loudness = 1.0
    for dim, parts in shards:
        steps = jax.random.uniform(jax.random.fold_in(jax.random.fold_in(own_key, 6), dim), (parts,), jnp.float32, least / len(shards), high / len(shards))
        loudness = loudness * jnp.repeat(jnp.exp(steps), extent[dim] // parts).reshape((-1,) + (1,) * (len(extent) - 1 - dim))
    return loudness


def gaussian(own_key, dims, scale, limit, pieces=(), held_as=jnp.bfloat16):
    result = scale * jax.random.normal(own_key, dims, jnp.float32)
    if pieces:
        result = result * levels(own_key, dims, pieces, -0.22, 0.18)
    return jnp.clip(result, -limit, limit).astype(held_as)


def setup_inputs(seed: int = 0) -> dict:
    key_of = jax.random.split(jax.random.key(seed), 10)
    schur_x = draw_schur_x(jax.random.fold_in(key_of[9], 71), 0)
    schur_y = draw_schur_y(jax.random.fold_in(key_of[9], 71), 0)
    residual_x = draw_residual_x(jax.random.fold_in(key_of[9], 71), 0)
    residual_y = draw_residual_y(jax.random.fold_in(key_of[9], 71), 0)
    basis_x = gaussian(key_of[4], (2 * SUBX, SUBY, PC, F), 0.15, 0.9, ((0, 32), (1, 16)), jnp.float32)
    basis_y = gaussian(key_of[5], (SUBX, 2 * SUBY, PC, F), 0.15, 0.9, ((0, 32), (1, 16)), jnp.float32)
    couple_x = jnp.clip(-0.3 + 0.4 * jax.random.uniform(key_of[6], (SUBX, SUBY, PC, PC), jnp.float32) ** levels(key_of[6], (SUBX, SUBY, PC, PC), ((0, 32), (1, 16)), -0.2, 0.2), -0.3, 0.1)
    couple_y = jnp.clip(-0.3 + 0.4 * jax.random.uniform(key_of[7], (SUBX, SUBY, PC, PC), jnp.float32) ** levels(key_of[7], (SUBX, SUBY, PC, PC), ((0, 32), (1, 16)), -0.2, 0.2), -0.3, 0.1)
    coarse_shift = jnp.clip(jnp.exp(math.log(0.5) - 2.3025851 * jax.random.uniform(key_of[8], (SUBX, SUBY, PC), jnp.float32) ** levels(key_of[8], (SUBX, SUBY, PC), ((0, 32), (1, 16)), -0.2, 0.2)), 0.05, 0.5)
    return dict(schur_x=schur_x, schur_y=schur_y, residual_x=residual_x, residual_y=residual_y, basis_x=basis_x, basis_y=basis_y, couple_x=couple_x, couple_y=couple_y, coarse_shift=coarse_shift)


HIGH = lax.Precision.HIGHEST

def face_average(s_low, s_high, r_low, r_high):
    summed = s_low + s_high
    factor = jnp.linalg.cholesky(summed)
    right_side = jnp.dot(s_low, r_low.T, precision=HIGH) + jnp.dot(s_high, r_high.T, precision=HIGH)
    forward = jax.scipy.linalg.solve_triangular(factor, right_side, lower=True)
    solved = jax.scipy.linalg.solve_triangular(factor, forward, lower=True, trans=1)
    return solved.T

def reference(schur_x, schur_y, residual_x, residual_y, basis_x, basis_y, couple_x, couple_y, coarse_shift):
    blocks_x = schur_x.reshape(SUBX, 2, SUBY, F, F)
    resid_bx = residual_x.reshape(SUBX, 2, SUBY, R, F)
    basis_bx = basis_x.reshape(SUBX, 2, SUBY, PC, F)
    blocks_y = schur_y.reshape(SUBX, SUBY, 2, F, F)
    resid_by = residual_y.reshape(SUBX, SUBY, 2, R, F)
    basis_by = basis_y.reshape(SUBX, SUBY, 2, PC, F)

    def pair_x(index):
        row_pos = index // SUBY
        col_pos = index % SUBY
        return face_average(blocks_x[row_pos, 1, col_pos], blocks_x[row_pos + 1, 0, col_pos], resid_bx[row_pos, 1, col_pos], resid_bx[row_pos + 1, 0, col_pos])

    def pair_y(index):
        row_pos = index // (SUBY - 1)
        col_pos = index % (SUBY - 1)
        return face_average(blocks_y[row_pos, col_pos, 1], blocks_y[row_pos, col_pos + 1, 0], resid_by[row_pos, col_pos, 1], resid_by[row_pos, col_pos + 1, 0])
    faces_x = lax.map(pair_x, jnp.arange((SUBX - 1) * SUBY, dtype=jnp.int32)).reshape(SUBX - 1, SUBY, R, F)
    faces_y = lax.map(pair_y, jnp.arange(SUBX * (SUBY - 1), dtype=jnp.int32)).reshape(SUBX, SUBY - 1, R, F)
    lower_x = jnp.concatenate([resid_bx[:1, 0], faces_x], axis=0)
    upper_x = jnp.concatenate([faces_x, resid_bx[-1:, 1]], axis=0)
    lower_y = jnp.concatenate([resid_by[:, :1, 0], faces_y], axis=1)
    upper_y = jnp.concatenate([faces_y, resid_by[:, -1:, 1]], axis=1)
    rhs_coarse = jnp.einsum('isjpf,isjrf->ijpr', basis_bx, resid_bx, precision=HIGH)
    rhs_coarse = rhs_coarse + jnp.einsum('ijspf,ijsrf->ijpr', basis_by, resid_by, precision=HIGH)
    mask_x = (jnp.arange(SUBX, dtype=jnp.int32) > 0).astype(jnp.float32)
    mask_y = (jnp.arange(SUBY, dtype=jnp.int32) > 0).astype(jnp.float32)
    link_x = couple_x * mask_x[:, None, None, None]
    link_y = couple_y * mask_y[None, :, None, None]
    next_x = jnp.concatenate([link_x[1:], jnp.zeros((1, SUBY, PC, PC), jnp.float32)], axis=0)
    next_y = jnp.concatenate([link_y[:, 1:], jnp.zeros((SUBX, 1, PC, PC), jnp.float32)], axis=1)
    diagonal = jnp.sum(jnp.abs(link_x), axis=2) + jnp.sum(jnp.abs(next_x), axis=3) + jnp.sum(jnp.abs(link_y), axis=2) + jnp.sum(jnp.abs(next_y), axis=3) + coarse_shift

    def operate(field):
        zero_x = jnp.zeros((1, SUBY, PC, R), jnp.float32)
        zero_y = jnp.zeros((SUBX, 1, PC, R), jnp.float32)
        prev_fx = jnp.concatenate([zero_x, field[:-1]], axis=0)
        next_fx = jnp.concatenate([field[1:], zero_x], axis=0)
        prev_fy = jnp.concatenate([zero_y, field[:, :-1]], axis=1)
        next_fy = jnp.concatenate([field[:, 1:], zero_y], axis=1)
        image = diagonal[..., None] * field
        image = image + jnp.einsum('ijab,ijar->ijbr', link_x, prev_fx, precision=HIGH)
        image = image + jnp.einsum('ijab,ijbr->ijar', next_x, next_fx, precision=HIGH)
        image = image + jnp.einsum('ijab,ijar->ijbr', link_y, prev_fy, precision=HIGH)
        image = image + jnp.einsum('ijab,ijbr->ijar', next_y, next_fy, precision=HIGH)
        return image
    coarse = jnp.zeros_like(rhs_coarse)
    remain = rhs_coarse
    direction = rhs_coarse
    norm_now = jnp.sum(remain * remain, axis=(0, 1, 2))
    for sweep_index in range(CITERS):
        image = operate(direction)
        alpha = norm_now / jnp.sum(direction * image, axis=(0, 1, 2))
        coarse = coarse + alpha * direction
        remain = remain - alpha * image
        norm_next = jnp.sum(remain * remain, axis=(0, 1, 2))
        direction = remain + norm_next / norm_now * direction
        norm_now = norm_next
    out_x = jnp.stack([lower_x, upper_x], axis=1)
    out_x = out_x + jnp.einsum('ijpr,isjpf->isjrf', coarse, basis_bx, precision=HIGH)
    out_y = jnp.stack([lower_y, upper_y], axis=2)
    out_y = out_y + jnp.einsum('ijpr,ijspf->ijsrf', coarse, basis_by, precision=HIGH)
    return (out_x.reshape(2 * SUBX, SUBY, R, F), out_y.reshape(SUBX, 2 * SUBY, R, F), coarse)
```

```python
import functools

import jax
import jax.numpy as jnp
from jax import lax
from jax.experimental import pallas as pl
from jax.experimental.pallas import tpu as pltpu
from jax.sharding import PartitionSpec as P

CITERS = 8
HIGH = lax.Precision.HIGHEST
F = 512
R = 32
PC = 6
B = 128
PANELS = F // B
LIMIT = 56 * 2**20
MESH = pl.DeviceIdType.MESH
CX, CY, SH = 24, 64, 104


def dot(a, b, ca=1, cb=0):
    return lax.dot_general(
        a, b, (((ca,), (cb,)), ((), ())), precision=HIGH, preferred_element_type=jnp.float32
    )


def panel_copies(source, target, send, recv, device):
    return [
        pltpu.make_async_remote_copy(
            src_ref=source.at[pl.ds(k * B, B), pl.ds(k * B, F - k * B)],
            dst_ref=target.at[pl.ds(k * B, B), pl.ds(k * B, F - k * B)],
            send_sem=send.at[k],
            recv_sem=recv.at[k],
            device_id=device,
            device_id_type=MESH,
        )
        for k in range(PANELS)
    ]


def flat_row(block, first, stride, width):
    rows, cols = block.shape
    lane = lax.broadcasted_iota(jnp.int32, (cols, width), 1) - first
    hot = jnp.where(
        (lane >= 0) & (lane < stride * rows) & (lane % stride == lax.broadcasted_iota(jnp.int32, (cols, width), 0)),
        1.0,
        0.0,
    )
    spread = dot(block, hot)
    lane = lax.broadcasted_iota(jnp.int32, (rows, width), 1) - first
    own = (lane >= 0) & (lane // stride == lax.broadcasted_iota(jnp.int32, (rows, width), 0))
    return jnp.sum(jnp.where(own, spread, 0.0), axis=0, keepdims=True)


def b_row(b):
    parts = []
    for tile in range(2):
        lane = lax.broadcasted_iota(jnp.int32, (R, B), 1)
        column = 16 * tile + 4 * (lane // 32) + lane % 4
        hot = jnp.where(column == lax.broadcasted_iota(jnp.int32, (R, B), 0), 1.0, 0.0)
        spread = dot(b, hot)
        lane = lax.broadcasted_iota(jnp.int32, (PC, B), 1)
        own = (lane % 32) // 4 == lax.broadcasted_iota(jnp.int32, (PC, B), 0)
        parts.append(jnp.sum(jnp.where(own, spread, 0.0), axis=0, keepdims=True))
    return parts


def send_round(source_of, target, send, recv, mine, device_of):
    copies = []
    for d in range(1, 8):
        other = lax.rem(mine + d, 8)
        copies.append(
            pltpu.make_async_remote_copy(
                src_ref=source_of(other),
                dst_ref=target.at[mine],
                send_sem=send.at[d],
                recv_sem=recv.at[d],
                device_id=device_of(other),
                device_id_type=MESH,
            )
        )
    for copy in copies:
        copy.start()
    return copies


def rows8(values):
    return jnp.concatenate([values, values], axis=0)


def conjugate_gradients(table, nexts, diag, coarse, remain, search):
    nexts[0:40, :] = pltpu.roll(table[CX : CX + 40, :], F - 1, 1)
    nexts[40:80, :] = pltpu.roll(table[CY : CY + 40, :], F - 32, 1)

    def link(base, a, b):
        return jnp.broadcast_to(table[base + 6 * a + b : base + 6 * a + b + 1, :], (8, F))

    def beyond(base, a, b):
        return jnp.broadcast_to(nexts[base + 6 * a + b : base + 6 * a + b + 1, :], (8, F))

    for k in range(PC):
        total = jnp.broadcast_to(table[SH + k : SH + k + 1, :], (8, F))
        for a in range(PC):
            total += jnp.abs(link(CX, a, k)) + jnp.abs(link(CY, a, k))
            total += jnp.abs(beyond(0, k, a)) + jnp.abs(beyond(40, k, a))
        diag[8 * k : 8 * k + 8, :] = total
        start = rows8(table[4 * k : 4 * k + 4, :])
        coarse[8 * k : 8 * k + 8, :] = jnp.zeros((8, F), jnp.float32)
        remain[8 * k : 8 * k + 8, :] = start
        search[8 * k : 8 * k + 8, :] = start

    def total_of(left, right):
        product = left * right
        part = product[0:8]
        for k in range(1, PC):
            part += product[8 * k : 8 * k + 8]
        part = (part[:, 0:128] + part[:, 128:256]) + (part[:, 256:384] + part[:, 384:512])
        return jnp.broadcast_to(jnp.sum(part, axis=1, keepdims=True), (8, F))

    def sweep(step, now):
        p = search[...]
        low_x, high_x = pltpu.roll(p, 1, 1), pltpu.roll(p, F - 1, 1)
        low_y, high_y = pltpu.roll(p, 32, 1), pltpu.roll(p, F - 32, 1)
        images = []
        for k in range(PC):
            image = diag[8 * k : 8 * k + 8, :] * p[8 * k : 8 * k + 8]
            for a in range(PC):
                rows = slice(8 * a, 8 * a + 8)
                image += link(CX, a, k) * low_x[rows] + beyond(0, k, a) * high_x[rows]
                image += link(CY, a, k) * low_y[rows] + beyond(40, k, a) * high_y[rows]
            images.append(image)
        image = jnp.concatenate(images, axis=0)
        alpha = jnp.concatenate([now / total_of(p, image)] * PC, axis=0)
        coarse[...] += alpha * p
        left = remain[...] - alpha * image
        remain[...] = left
        new = total_of(left, left)
        search[...] = left + jnp.concatenate([new / now] * PC, axis=0) * p
        return new

    first = remain[...]
    lax.fori_loop(0, CITERS, sweep, total_of(first, first))


def exchange(
    schur_x, schur_y, residual_x, residual_y, basis_x, basis_y, couple_x, couple_y, shift,
    sum_x, sum_y, side_x, side_y, coarse_t,
    high_x, high_y, local_x, local_y, out_tx, out_ty, in_tx, in_ty,
    msg, near, plane, slabs, whole, table, nexts, diag, coarse, remain, search, back, home,
    load_sem, sx_send, sx_recv, sy_send, sy_recv, t_send, t_recv,
    a_send, a_recv, b_send, b_recv, c_send, c_recv, d_send, d_recv,
):
    i, j = lax.axis_index("sx"), lax.axis_index("sy")
    x_low, x_high = (lax.rem(i + 31, 32), j), (lax.rem(i + 1, 32), j)
    y_low, y_high = (i, lax.rem(j + 15, 16)), (i, lax.rem(j + 1, 16))
    q, y, z = lax.rem(i, 8), lax.rem(j, 2) * 4 + i // 8, j // 2

    def near_of(other):
        return ((i // 8) * 8 + other, j)

    def plane_of(other):
        return (lax.rem(other, 4) * 8 + q, z * 2 + other // 4)

    def stack_of(other):
        return (i, other * 2 + lax.rem(j, 2))

    loads = []
    for s, (source, target) in enumerate(
        ((schur_y.at[0, 0], local_y.at[0]), (schur_x.at[0, 0], local_x.at[0]),
         (schur_x.at[1, 0], local_x.at[1]), (schur_y.at[0, 1], local_y.at[1]))
    ):
        copy = pltpu.make_async_copy(source, target, load_sem.at[s])
        copy.start()
        loads.append(copy)

    barrier = pltpu.get_barrier_semaphore()
    for device in (x_low, x_high, y_low, y_high):
        pl.semaphore_signal(barrier, inc=1, device_id=device, device_id_type=MESH)
    for d in range(1, 8):
        for mine, device_of in ((q, near_of), (y, plane_of), (z, stack_of)):
            pl.semaphore_signal(
                barrier, inc=1, device_id=device_of(lax.rem(mine + d, 8)), device_id_type=MESH
            )
    pl.semaphore_wait(barrier, 25)

    blocks_y = panel_copies(schur_y.at[0, 0], high_y, sy_send, sy_recv, y_low)
    blocks_x = panel_copies(schur_x.at[0, 0], high_x, sx_send, sx_recv, x_low)
    for copy in blocks_y + blocks_x:
        copy.start()

    b = dot(basis_x[0, 0], residual_x[0, 0], 1, 1) + dot(basis_x[1, 0], residual_x[1, 0], 1, 1)
    b += dot(basis_y[0, 0], residual_y[0, 0], 1, 1) + dot(basis_y[0, 1], residual_y[0, 1], 1, 1)
    b_tiles = b_row(b)
    keep_x, keep_y = (i > 0).astype(jnp.float32), (j > 0).astype(jnp.float32)
    links = flat_row(couple_x[0, 0] * keep_x, CX, PC, B) + flat_row(couple_y[0, 0] * keep_y, CY, PC, B)
    links += flat_row(shift[0], SH, PC, B)
    row = jnp.concatenate(b_tiles + [links], axis=1)
    msg[...] = jnp.broadcast_to(row, (8, 3 * B))
    near[q] = msg[...]
    copies = send_round(lambda other: msg, near, a_send, a_recv, q, near_of)
    for copy in copies:
        copy.wait()
    sub = lax.broadcasted_iota(jnp.int32, (8, 3 * B), 0)
    rows = jnp.zeros((8, 3 * B), jnp.float32)
    for s in range(8):
        rows = jnp.where(sub == s, near[s], rows)
    plane[y] = rows
    copies = send_round(lambda other: plane.at[y], plane, b_send, b_recv, y, plane_of)

    loads[0].wait()
    out_ty[...] = dot(residual_y[0, 0], local_y[0])
    t_y = pltpu.make_async_remote_copy(
        src_ref=out_ty, dst_ref=in_ty, send_sem=t_send.at[0], recv_sem=t_recv.at[0],
        device_id=y_low, device_id_type=MESH,
    )
    t_y.start()
    loads[1].wait()
    out_tx[...] = dot(residual_x[0, 0], local_x[0])
    t_x = pltpu.make_async_remote_copy(
        src_ref=out_tx, dst_ref=in_tx, send_sem=t_send.at[1], recv_sem=t_recv.at[1],
        device_id=x_low, device_id_type=MESH,
    )
    t_x.start()

    for copy in copies:
        copy.wait()
    lane = lax.broadcasted_iota(jnp.int32, (64, B), 1)
    data = plane[...].reshape(64, 3 * B)
    for s in range(8):
        tile = data[:, B * (s // 4) : B * (s // 4) + B]
        if s % 4:
            tile = pltpu.roll(tile, B - 32 * (s % 4), 1)
        slabs[s] = jnp.where(lane < 24, tile, data[:, 2 * B : 3 * B])
    whole[z] = slabs[z]
    copies = send_round(lambda other: slabs.at[other], whole, c_send, c_recv, z, stack_of)

    loads[2].wait()
    side_x[...] = dot(residual_x[1, 0], local_x[1])
    loads[3].wait()
    side_y[...] = dot(residual_y[0, 1], local_y[1])

    for copy in copies:
        copy.wait()
    for s in range(4):
        table[:, s * B : s * B + B] = whole[2 * s : 2 * s + 2].reshape(B, B).T
    conjugate_gradients(table, nexts, diag, coarse, remain, search)

    lane = lax.broadcasted_iota(jnp.int32, (8, B), 1)
    place = y * 8 + q
    for s in range(4):
        first = jnp.zeros((8, B), jnp.float32)
        second = first
        for k in range(PC):
            part = pltpu.roll(coarse[8 * k : 8 * k + 8, s * B : s * B + B], B - place, 1)
            first = jnp.where(lane == k, jnp.broadcast_to(part[:, 0:1], (8, B)), first)
            second = jnp.where(lane == k, jnp.broadcast_to(part[:, 64:65], (8, B)), second)
        back[2 * s] = first
        back[2 * s + 1] = second
    home[z] = back[z]
    copies = send_round(lambda other: back.at[other], home, d_send, d_recv, z, stack_of)
    for copy in copies:
        copy.wait()
    sub = lax.broadcasted_iota(jnp.int32, (8, B), 0)
    for s in range(4):
        coarse_t[8 * s : 8 * s + 8, :] = jnp.where(sub < 4, home[2 * s], home[2 * s + 1])

    t_x.wait()
    side_x[...] += in_tx[...]
    for k, copy in enumerate(blocks_x):
        copy.wait()
        rows, cols = slice(k * B, k * B + B), slice(k * B, F)
        sum_x[rows, cols] = high_x[rows, cols] + local_x[1, rows, cols]
    t_y.wait()
    side_y[...] += in_ty[...]
    for k, copy in enumerate(blocks_y):
        copy.wait()
        rows, cols = slice(k * B, k * B + B), slice(k * B, F)
        sum_y[rows, cols] = high_y[rows, cols] + local_y[1, rows, cols]


def spread(values):
    return jnp.broadcast_to(values, (8, B))


def panel(tiles_of, at, lane, sub, ahead):
    heads = [tiles[0] for tiles in tiles_of]
    columns = [[spread(head[:, at + c : at + c + 1]) for c in range(8)] for head in heads]
    for c in range(8):
        here = sub == c
        for f in range(len(heads)):
            own = columns[f][c]
            inverse = 1.0 / spread(own[c : c + 1, :])
            fresh = []
            for d in range(8):
                if d == c:
                    fresh.append(jnp.where(here, inverse, -own * inverse))
                else:
                    row = spread(columns[f][d][c : c + 1, :]) * inverse
                    fresh.append(jnp.where(here, row, columns[f][d] - own * row))
            row = spread(heads[f][c : c + 1, :]) * inverse
            heads[f] = jnp.where(here, row, heads[f] - own * row)
            columns[f] = fresh
    inside = (lane >= at) & (lane < at + 8)
    results = []
    for f, tiles in enumerate(tiles_of):
        head = heads[f]
        for c in range(8):
            head = jnp.where(lane == at + c, columns[f][c], head)
        result = [head]
        for t in range(1, 1 + ahead):
            parts = [
                spread(tiles[t][:, at + c : at + c + 1]) * spread(head[c : c + 1, :])
                for c in range(8)
            ]
            total = ((parts[0] + parts[1]) + (parts[2] + parts[3])) + (
                (parts[4] + parts[5]) + (parts[6] + parts[7])
            )
            result.append(jnp.where(inside, 0.0, tiles[t]) - total)
        rest = jnp.concatenate(tiles[1 + ahead :], axis=0)
        update = dot(rest[:, at : at + 8], head)
        for t in range(1 + ahead, len(tiles)):
            row = (t - 1 - ahead) * 8
            result.append(jnp.where(inside, 0.0, tiles[t]) - update[row : row + 8, :])
        results.append(result)
    return results


def inverses(matrices, unroll=4, ahead=2):
    lane = lax.broadcasted_iota(jnp.int32, (8, B), 1)
    sub = lax.broadcasted_iota(jnp.int32, (8, B), 0)

    def body(step, carry):
        tiles_of = [list(tiles) for tiles in carry]
        for u in range(unroll):
            tiles_of = panel(tiles_of, 8 * u, lane, sub, ahead)
            tiles_of = [tiles[1:] + tiles[:1] for tiles in tiles_of]
        return tuple(
            tuple(pltpu.roll(tile, B - 8 * unroll, 1) for tile in tiles) for tiles in tiles_of
        )

    start = tuple(tuple(m[8 * t : 8 * t + 8, :] for t in range(B // 8)) for m in matrices)
    end = lax.fori_loop(0, B // 8 // unroll, body, start)
    return [jnp.concatenate(tiles, axis=0) for tiles in end]


def solve_faces(sums, sides, weights):
    for k in range(PANELS):
        own, rest = slice(k * B, k * B + B), slice(k * B + B, F)
        for a, side, w, inverse in zip(
            sums, sides, weights, inverses([a[own, own] for a in sums]), strict=True
        ):
            part = dot(side[:, own], inverse)
            if k < PANELS - 1:
                row = a[own, rest]
                weight = dot(inverse, row)
                w[own, rest] = weight
                for m in range(k + 1, PANELS):
                    at = (m - k - 1) * B
                    a[m * B : m * B + B, m * B :] -= dot(row[:, at : at + B], weight[:, at:], 0, 0)
                side[:, rest] -= dot(part, row)
            side[:, own] = part
    for k in range(PANELS - 2, -1, -1):
        own, rest = slice(k * B, k * B + B), slice(k * B + B, F)
        for side, w in zip(sides, weights, strict=True):
            side[:, own] -= dot(side[:, rest], w[own, rest], 1, 1)


def solve(sum_x, sum_y, side_x, side_y, face_x, face_y, work_x, work_y, weight_x, weight_y):
    for source, target in ((sum_x, work_x), (sum_y, work_y)):
        for k in range(PANELS):
            rows, cols = slice(k * B, k * B + B), slice(k * B, F)
            target[rows, cols] = source[rows, cols]
    face_x[...] = side_x[...]
    face_y[...] = side_y[...]
    solve_faces((work_x, work_y), (face_x, face_y), (weight_x, weight_y))


def lifted(coarse_t, basis):
    total = coarse_t[:, 0:1] * basis[0:1, :]
    for k in range(1, PC):
        total += coarse_t[:, k : k + 1] * basis[k : k + 1, :]
    return total


def finish(
    face_x, face_y, residual_x, residual_y, basis_x, basis_y, coarse_t,
    out_x, out_y, values, low_x, low_y, send, recv,
):
    i, j = lax.axis_index("sx"), lax.axis_index("sy")
    x_low, x_high = (lax.rem(i + 31, 32), j), (lax.rem(i + 1, 32), j)
    y_low, y_high = (i, lax.rem(j + 15, 16)), (i, lax.rem(j + 1, 16))
    barrier = pltpu.get_barrier_semaphore()
    for device in (x_low, x_high, y_low, y_high):
        pl.semaphore_signal(barrier, inc=1, device_id=device, device_id_type=MESH)
    pl.semaphore_wait(barrier, 4)
    copies = [
        pltpu.make_async_remote_copy(
            src_ref=source, dst_ref=target, send_sem=send.at[s], recv_sem=recv.at[s],
            device_id=device, device_id_type=MESH,
        )
        for s, (source, target, device) in enumerate(
            ((face_y, low_y, y_high), (face_x, low_x, x_high))
        )
    ]
    for copy in copies:
        copy.start()
    c = coarse_t[...]
    values[0, 0] = jnp.concatenate([c] * 4, axis=0).T[0:PC, 0:R]
    out_x[1, 0] = jnp.where(i == 31, residual_x[1, 0], face_x[...]) + lifted(c, basis_x[1, 0])
    out_y[0, 1] = jnp.where(j == 15, residual_y[0, 1], face_y[...]) + lifted(c, basis_y[0, 1])
    copies[1].wait()
    out_x[0, 0] = jnp.where(i == 0, residual_x[0, 0], low_x[...]) + lifted(c, basis_x[0, 0])
    copies[0].wait()
    out_y[0, 0] = jnp.where(j == 0, residual_y[0, 0], low_y[...]) + lifted(c, basis_y[0, 0])


def f32(*shape):
    return jax.ShapeDtypeStruct(shape, jnp.float32)


def vmem(*shape):
    return pltpu.VMEM(shape, jnp.float32)


HBM = pl.BlockSpec(memory_space=pl.ANY)
LOCAL = pl.BlockSpec(memory_space=pltpu.VMEM)


def shards(
    schur_x, schur_y, residual_x, residual_y, basis_x, basis_y, couple_x, couple_y, coarse_shift
):
    dma = pltpu.SemaphoreType.DMA
    sum_x, sum_y, side_x, side_y, coarse_t = pl.pallas_call(
        exchange,
        name="exchange",
        out_shape=(f32(F, F), f32(F, F), f32(R, F), f32(R, F), f32(R, B)),
        in_specs=[HBM] * 2 + [LOCAL] * 7,
        out_specs=(LOCAL,) * 5,
        scratch_shapes=[
            vmem(F, F), vmem(F, F), vmem(2, F, F), vmem(2, F, F),
            vmem(R, F), vmem(R, F), vmem(R, F), vmem(R, F),
            vmem(8, 3 * B), vmem(8, 8, 3 * B), vmem(8, 8, 3 * B), vmem(8, 64, B), vmem(8, 64, B),
            vmem(B, F), vmem(80, F), vmem(8 * PC, F), vmem(8 * PC, F), vmem(8 * PC, F),
            vmem(8 * PC, F), vmem(8, 8, B), vmem(8, 8, B),
            dma((4,)), dma((4,)), dma((4,)), dma((4,)), dma((4,)), dma((2,)), dma((2,)),
        ] + [dma((8,))] * 8,
        compiler_params=pltpu.CompilerParams(
            collective_id=0, has_side_effects=True, vmem_limit_bytes=LIMIT
        ),
    )(schur_x, schur_y, residual_x, residual_y, basis_x, basis_y, couple_x, couple_y, coarse_shift)
    face_x, face_y = pl.pallas_call(
        solve,
        name="solve",
        out_shape=(f32(R, F), f32(R, F)),
        in_specs=[LOCAL] * 4,
        out_specs=(LOCAL,) * 2,
        scratch_shapes=[vmem(F, F)] * 4,
        compiler_params=pltpu.CompilerParams(vmem_limit_bytes=LIMIT),
    )(sum_x, sum_y, side_x, side_y)
    return pl.pallas_call(
        finish,
        name="finish",
        out_shape=(f32(2, 1, R, F), f32(1, 2, R, F), f32(1, 1, PC, R)),
        in_specs=[LOCAL] * 7,
        out_specs=(LOCAL,) * 3,
        scratch_shapes=[vmem(R, F), vmem(R, F), dma((2,)), dma((2,))],
        compiler_params=pltpu.CompilerParams(
            collective_id=1, has_side_effects=True, vmem_limit_bytes=LIMIT
        ),
    )(face_x, face_y, residual_x, residual_y, basis_x, basis_y, coarse_t)


def solution(mesh):
    cells = P("sx", "sy", None, None)
    return jax.shard_map(
        shards,
        mesh=mesh,
        in_specs=(cells,) * 8 + (P("sx", "sy", None),),
        out_specs=(cells,) * 3,
        check_vma=False,
    )
```

```python
import functools

import jax
import jax.numpy as jnp
from jax import lax
from jax.experimental import pallas as pl
from jax.experimental.pallas import tpu as pltpu
from jax.sharding import PartitionSpec as P

CITERS = 8
HIGH = lax.Precision.HIGHEST
F = 512
R = 32
PC = 6
B = 128
PANELS = F // B
LIMIT = 56 * 2**20
MESH = pl.DeviceIdType.MESH
CX, CY, SH = 24, 64, 104
BETWEEN = 2


def dot(a, b, ca=1, cb=0):
    return lax.dot_general(
        a, b, (((ca,), (cb,)), ((), ())), precision=HIGH, preferred_element_type=jnp.float32
    )


def panel_copies(source, target, send, recv, device):
    return [
        pltpu.make_async_remote_copy(
            src_ref=source.at[pl.ds(k * B, B), pl.ds(k * B, F - k * B)],
            dst_ref=target.at[pl.ds(k * B, B), pl.ds(k * B, F - k * B)],
            send_sem=send.at[k],
            recv_sem=recv.at[k],
            device_id=device,
            device_id_type=MESH,
        )
        for k in range(PANELS)
    ]


def flat_row(block, first, stride, width):
    rows, cols = block.shape
    lane = lax.broadcasted_iota(jnp.int32, (cols, width), 1) - first
    hot = jnp.where(
        (lane >= 0) & (lane < stride * rows) & (lane % stride == lax.broadcasted_iota(jnp.int32, (cols, width), 0)),
        1.0,
        0.0,
    )
    spread = dot(block, hot)
    lane = lax.broadcasted_iota(jnp.int32, (rows, width), 1) - first
    own = (lane >= 0) & (lane // stride == lax.broadcasted_iota(jnp.int32, (rows, width), 0))
    return jnp.sum(jnp.where(own, spread, 0.0), axis=0, keepdims=True)


def b_row(b):
    parts = []
    for tile in range(2):
        lane = lax.broadcasted_iota(jnp.int32, (R, B), 1)
        column = 16 * tile + 4 * (lane // 32) + lane % 4
        hot = jnp.where(column == lax.broadcasted_iota(jnp.int32, (R, B), 0), 1.0, 0.0)
        spread = dot(b, hot)
        lane = lax.broadcasted_iota(jnp.int32, (8, B), 1)
        own = (lane % 32) // 4 == lax.broadcasted_iota(jnp.int32, (8, B), 0)
        parts.append(jnp.sum(jnp.where(own, spread, 0.0), axis=0, keepdims=True))
    return parts


def send_round(source_of, target, send, recv, mine, device_of):
    copies = []
    for d in range(1, 8):
        other = lax.rem(mine + d, 8)
        copies.append(
            pltpu.make_async_remote_copy(
                src_ref=source_of(other),
                dst_ref=target.at[mine],
                send_sem=send.at[d],
                recv_sem=recv.at[d],
                device_id=device_of(other),
                device_id_type=MESH,
            )
        )
    for copy in copies:
        copy.start()
    return copies


def rows8(values):
    return jnp.concatenate([values, values], axis=0)


def conjugate_gradients(table, nexts, diag, coarse, remain, search):
    nexts[0:40, :] = pltpu.roll(table[CX : CX + 40, :], F - 1, 1)
    nexts[40:80, :] = pltpu.roll(table[CY : CY + 40, :], F - 32, 1)

    def link(base, a, b):
        return jnp.broadcast_to(table[base + 6 * a + b : base + 6 * a + b + 1, :], (8, F))

    def beyond(base, a, b):
        return jnp.broadcast_to(nexts[base + 6 * a + b : base + 6 * a + b + 1, :], (8, F))

    for k in range(PC):
        total = jnp.broadcast_to(table[SH + k : SH + k + 1, :], (8, F))
        for a in range(PC):
            total += jnp.abs(link(CX, a, k)) + jnp.abs(link(CY, a, k))
            total += jnp.abs(beyond(0, k, a)) + jnp.abs(beyond(40, k, a))
        diag[8 * k : 8 * k + 8, :] = total
        start = rows8(table[4 * k : 4 * k + 4, :])
        coarse[8 * k : 8 * k + 8, :] = jnp.zeros((8, F), jnp.float32)
        remain[8 * k : 8 * k + 8, :] = start
        search[8 * k : 8 * k + 8, :] = start

    def total_of(left, right):
        product = left * right
        part = product[0:8]
        for k in range(1, PC):
            part += product[8 * k : 8 * k + 8]
        part = (part[:, 0:128] + part[:, 128:256]) + (part[:, 256:384] + part[:, 384:512])
        return jnp.broadcast_to(jnp.sum(part, axis=1, keepdims=True), (8, F))

    def sweep(step, now):
        p = search[...]
        low_x, high_x = pltpu.roll(p, 1, 1), pltpu.roll(p, F - 1, 1)
        low_y, high_y = pltpu.roll(p, 32, 1), pltpu.roll(p, F - 32, 1)
        images = []
        for k in range(PC):
            image = diag[8 * k : 8 * k + 8, :] * p[8 * k : 8 * k + 8]
            for a in range(PC):
                rows = slice(8 * a, 8 * a + 8)
                image += link(CX, a, k) * low_x[rows] + beyond(0, k, a) * high_x[rows]
                image += link(CY, a, k) * low_y[rows] + beyond(40, k, a) * high_y[rows]
            images.append(image)
        image = jnp.concatenate(images, axis=0)
        alpha = jnp.concatenate([now / total_of(p, image)] * PC, axis=0)
        coarse[...] += alpha * p
        left = remain[...] - alpha * image
        remain[...] = left
        new = total_of(left, left)
        search[...] = left + jnp.concatenate([new / now] * PC, axis=0) * p
        return new

    first = remain[...]
    lax.fori_loop(0, CITERS, sweep, total_of(first, first))


def spread(values):
    return jnp.broadcast_to(values, (8, B))


def panel(tiles_of, at, lane, sub, ahead):
    heads = [tiles[0] for tiles in tiles_of]
    columns = [[spread(head[:, at + c : at + c + 1]) for c in range(8)] for head in heads]
    for c in range(8):
        here = sub == c
        for f in range(len(heads)):
            own = columns[f][c]
            inverse = 1.0 / spread(own[c : c + 1, :])
            fresh = []
            for d in range(8):
                if d == c:
                    fresh.append(jnp.where(here, inverse, -own * inverse))
                else:
                    row = spread(columns[f][d][c : c + 1, :]) * inverse
                    fresh.append(jnp.where(here, row, columns[f][d] - own * row))
            row = spread(heads[f][c : c + 1, :]) * inverse
            heads[f] = jnp.where(here, row, heads[f] - own * row)
            columns[f] = fresh
    inside = (lane >= at) & (lane < at + 8)
    results = []
    for f, tiles in enumerate(tiles_of):
        head = heads[f]
        for c in range(8):
            head = jnp.where(lane == at + c, columns[f][c], head)
        result = [head]
        for t in range(1, 1 + ahead):
            parts = [
                spread(tiles[t][:, at + c : at + c + 1]) * spread(head[c : c + 1, :])
                for c in range(8)
            ]
            total = ((parts[0] + parts[1]) + (parts[2] + parts[3])) + (
                (parts[4] + parts[5]) + (parts[6] + parts[7])
            )
            result.append(jnp.where(inside, 0.0, tiles[t]) - total)
        rest = jnp.concatenate(tiles[1 + ahead :], axis=0)
        update = dot(rest[:, at : at + 8], head)
        for t in range(1 + ahead, len(tiles)):
            row = (t - 1 - ahead) * 8
            result.append(jnp.where(inside, 0.0, tiles[t]) - update[row : row + 8, :])
        results.append(result)
    return results


def inverses(matrices, unroll=4, ahead=2):
    lane = lax.broadcasted_iota(jnp.int32, (8, B), 1)
    sub = lax.broadcasted_iota(jnp.int32, (8, B), 0)

    def body(step, carry):
        tiles_of = [list(tiles) for tiles in carry]
        for u in range(unroll):
            tiles_of = panel(tiles_of, 8 * u, lane, sub, ahead)
            tiles_of = [tiles[1:] + tiles[:1] for tiles in tiles_of]
        return tuple(
            tuple(pltpu.roll(tile, B - 8 * unroll, 1) for tile in tiles) for tiles in tiles_of
        )

    start = tuple(tuple(m[8 * t : 8 * t + 8, :] for t in range(B // 8)) for m in matrices)
    end = lax.fori_loop(0, B // 8 // unroll, body, start)
    return [jnp.concatenate(tiles, axis=0) for tiles in end]


def solve_faces(sums, highs, arrivals, sides, weights, between):
    for k in range(PANELS):
        own, rest = slice(k * B, k * B + B), slice(k * B + B, F)
        for a, high, copies in zip(sums, highs, arrivals, strict=True):
            copies[k].wait()
            a[own, k * B :] += high[own, k * B :]
        for a, side, w, inverse in zip(
            sums, sides, weights, inverses([a[own, own] for a in sums]), strict=True
        ):
            part = dot(side[:, own], inverse)
            if k < PANELS - 1:
                row = a[own, rest]
                weight = dot(inverse, row)
                w[own, rest] = weight
                for m in range(k + 1, PANELS):
                    at = (m - k - 1) * B
                    a[m * B : m * B + B, m * B :] -= dot(row[:, at : at + B], weight[:, at:], 0, 0)
                side[:, rest] -= dot(part, row)
            side[:, own] = part
        between(k)
    for k in range(PANELS - 2, -1, -1):
        own, rest = slice(k * B, k * B + B), slice(k * B + B, F)
        for side, w in zip(sides, weights, strict=True):
            side[:, own] -= dot(side[:, rest], w[own, rest], 1, 1)


def lifted(coarse_t, rows):
    total = coarse_t[:, 0:1] * rows[0]
    for k in range(1, PC):
        total += coarse_t[:, k : k + 1] * rows[k]
    return total


def apply(
    schur_x, schur_y, residual_x, residual_y, basis_x, basis_y, couple_x, couple_y, shift,
    out_x, out_y, values,
    high_x, high_y, local_x, local_y, weight_x, weight_y, side_x, side_y, low_x, low_y,
    out_tx, out_ty, in_tx, in_ty,
    msg, near, plane, slabs, whole, table, nexts, diag, coarse, remain, search, back, home,
    load_sem, sx_send, sx_recv, sy_send, sy_recv, t_send, t_recv, u_send, u_recv,
    a_send, a_recv, b_send, b_recv, c_send, c_recv, d_send, d_recv,
):
    i, j = lax.axis_index("sx"), lax.axis_index("sy")
    x_low, x_high = (lax.rem(i + 31, 32), j), (lax.rem(i + 1, 32), j)
    y_low, y_high = (i, lax.rem(j + 15, 16)), (i, lax.rem(j + 1, 16))
    q, y, z = lax.rem(i, 8), lax.rem(j, 2) * 4 + i // 8, j // 2

    def near_of(other):
        return ((i // 8) * 8 + other, j)

    def plane_of(other):
        return (lax.rem(other, 4) * 8 + q, z * 2 + other // 4)

    def stack_of(other):
        return (i, other * 2 + lax.rem(j, 2))

    loads = []
    for s, (source, target) in enumerate(
        ((schur_y.at[0, 0], local_y.at[0]), (schur_x.at[0, 0], local_x.at[0]),
         (schur_x.at[1, 0], local_x.at[1]), (schur_y.at[0, 1], local_y.at[1]))
    ):
        copy = pltpu.make_async_copy(source, target, load_sem.at[s])
        copy.start()
        loads.append(copy)

    barrier = pltpu.get_barrier_semaphore()
    for device in (x_low, x_high, y_low, y_high):
        pl.semaphore_signal(barrier, inc=1, device_id=device, device_id_type=MESH)
    for d in range(1, 8):
        for mine, device_of in ((q, near_of), (y, plane_of), (z, stack_of)):
            pl.semaphore_signal(
                barrier, inc=1, device_id=device_of(lax.rem(mine + d, 8)), device_id_type=MESH
            )
    pl.semaphore_wait(barrier, 25)

    blocks_y = panel_copies(schur_y.at[0, 0], high_y, sy_send, sy_recv, y_low)
    blocks_x = panel_copies(schur_x.at[0, 0], high_x, sx_send, sx_recv, x_low)
    blocks_y[0].start()
    blocks_x[0].start()

    def to_low(source, target, s, device):
        return pltpu.make_async_remote_copy(
            src_ref=source, dst_ref=target, send_sem=t_send.at[s], recv_sem=t_recv.at[s],
            device_id=device, device_id_type=MESH,
        )

    rows_x = [[basis_x[s, k] for k in range(PC)] for s in range(2)]
    rows_y = [[basis_y[0, k, s : s + 1, :] for k in range(PC)] for s in range(2)]
    pad = jnp.zeros((2, F), jnp.float32)
    b = jnp.zeros((8, R), jnp.float32)
    for rows, residual in (
        (rows_x[0], residual_x[0, 0]), (rows_x[1], residual_x[1, 0]),
        (rows_y[0], residual_y[0, 0]), (rows_y[1], residual_y[0, 1]),
    ):
        b += dot(jnp.concatenate(rows + [pad], axis=0), residual, 1, 1)
    b_tiles = b_row(b)
    keep_x, keep_y = (i > 0).astype(jnp.float32), (j > 0).astype(jnp.float32)
    link_x = jnp.concatenate([couple_x[0, a] for a in range(PC)], axis=0) * keep_x
    link_y = jnp.concatenate([couple_y[0, a] for a in range(PC)], axis=0) * keep_y
    links = flat_row(link_x, CX, PC, B) + flat_row(link_y, CY, PC, B) + flat_row(shift[0], SH, PC, B)
    msg[...] = jnp.broadcast_to(jnp.concatenate(b_tiles + [links], axis=1), (8, 3 * B))
    near[q] = msg[...]
    near_copies = send_round(lambda other: msg, near, a_send, a_recv, q, near_of)
    for copy in blocks_x[1:]:
        copy.start()

    loads[0].wait()
    out_ty[...] = dot(residual_y[0, 0], local_y[0])
    t_y = to_low(out_ty, in_ty, 0, y_low)
    t_y.start()
    loads[1].wait()
    out_tx[...] = dot(residual_x[0, 0], local_x[0])
    t_x = to_low(out_tx, in_tx, 1, x_low)
    t_x.start()

    for copy in near_copies:
        copy.wait()
    sub = lax.broadcasted_iota(jnp.int32, (8, 3 * B), 0)
    rows = jnp.zeros((8, 3 * B), jnp.float32)
    for s in range(8):
        rows = jnp.where(sub == s, near[s], rows)
    plane[y] = rows
    plane_copies = send_round(lambda other: plane.at[y], plane, b_send, b_recv, y, plane_of)
    for copy in blocks_y[1:]:
        copy.start()

    loads[2].wait()
    side_x[...] = dot(residual_x[1, 0], local_x[1])
    loads[3].wait()
    side_y[...] = dot(residual_y[0, 1], local_y[1])
    t_x.wait()
    side_x[...] += in_tx[...]
    t_y.wait()
    side_y[...] += in_ty[...]

    stack_copies = []

    def between(k):
        if k != BETWEEN:
            return
        for copy in plane_copies:
            copy.wait()
        lane = lax.broadcasted_iota(jnp.int32, (64, B), 1)
        data = plane[...].reshape(64, 3 * B)
        for s in range(8):
            tile = data[:, B * (s // 4) : B * (s // 4) + B]
            if s % 4:
                tile = pltpu.roll(tile, B - 32 * (s % 4), 1)
            slabs[s] = jnp.where(lane < 24, tile, data[:, 2 * B : 3 * B])
        whole[z] = slabs[z]
        stack_copies.extend(
            send_round(lambda other: slabs.at[other], whole, c_send, c_recv, z, stack_of)
        )

    solve_faces(
        (local_x.at[1], local_y.at[1]), (high_x, high_y), (blocks_x, blocks_y),
        (side_x, side_y), (weight_x, weight_y), between,
    )
    faces = [
        pltpu.make_async_remote_copy(
            src_ref=source, dst_ref=target, send_sem=u_send.at[s], recv_sem=u_recv.at[s],
            device_id=device, device_id_type=MESH,
        )
        for s, (source, target, device) in enumerate(
            ((side_y, low_y, y_high), (side_x, low_x, x_high))
        )
    ]
    for copy in faces:
        copy.start()

    for copy in stack_copies:
        copy.wait()
    for s in range(4):
        table[:, s * B : s * B + B] = whole[2 * s : 2 * s + 2].reshape(B, B).T
    conjugate_gradients(table, nexts, diag, coarse, remain, search)

    lane = lax.broadcasted_iota(jnp.int32, (8, B), 1)
    place = y * 8 + q
    for s in range(4):
        first = jnp.zeros((8, B), jnp.float32)
        second = first
        for k in range(PC):
            part = pltpu.roll(coarse[8 * k : 8 * k + 8, s * B : s * B + B], B - place, 1)
            first = jnp.where(lane == k, jnp.broadcast_to(part[:, 0:1], (8, B)), first)
            second = jnp.where(lane == k, jnp.broadcast_to(part[:, 64:65], (8, B)), second)
        back[2 * s] = first
        back[2 * s + 1] = second
    home[z] = back[z]
    home_copies = send_round(lambda other: back.at[other], home, d_send, d_recv, z, stack_of)
    for copy in home_copies:
        copy.wait()
    sub = lax.broadcasted_iota(jnp.int32, (8, B), 0)
    c = jnp.concatenate([jnp.where(sub < 4, home[2 * s], home[2 * s + 1]) for s in range(4)], axis=0)
    turned = jnp.concatenate([c] * 4, axis=0).T
    for k in range(PC):
        values[0, k] = turned[k : k + 1, 0:R]
    out_x[1, 0] = jnp.where(i == 31, residual_x[1, 0], side_x[...]) + lifted(c, rows_x[1])
    out_y[0, 1] = jnp.where(j == 15, residual_y[0, 1], side_y[...]) + lifted(c, rows_y[1])
    faces[1].wait()
    out_x[0, 0] = jnp.where(i == 0, residual_x[0, 0], low_x[...]) + lifted(c, rows_x[0])
    faces[0].wait()
    out_y[0, 0] = jnp.where(j == 0, residual_y[0, 0], low_y[...]) + lifted(c, rows_y[0])


def f32(*shape):
    return jax.ShapeDtypeStruct(shape, jnp.float32)


def vmem(*shape):
    return pltpu.VMEM(shape, jnp.float32)


HBM = pl.BlockSpec(memory_space=pl.ANY)
LOCAL = pl.BlockSpec(memory_space=pltpu.VMEM)


def shards(
    schur_x, schur_y, residual_x, residual_y, basis_x, basis_y, couple_x, couple_y, coarse_shift
):
    dma = pltpu.SemaphoreType.DMA

    def turn(array):
        return jnp.swapaxes(array, 1, 2)

    out_x, out_y, values = pl.pallas_call(
        apply,
        name="apply",
        out_shape=(f32(2, 1, R, F), f32(1, 2, R, F), f32(1, PC, 1, R)),
        in_specs=[HBM] * 2 + [LOCAL] * 7,
        out_specs=(LOCAL,) * 3,
        scratch_shapes=[
            vmem(F, F), vmem(F, F), vmem(2, F, F), vmem(2, F, F), vmem(F, F), vmem(F, F),
        ] + [vmem(R, F)] * 8 + [
            vmem(8, 3 * B), vmem(8, 8, 3 * B), vmem(8, 8, 3 * B), vmem(8, 64, B), vmem(8, 64, B),
            vmem(B, F), vmem(80, F), vmem(8 * PC, F), vmem(8 * PC, F), vmem(8 * PC, F),
            vmem(8 * PC, F), vmem(8, 8, B), vmem(8, 8, B),
            dma((4,)), dma((4,)), dma((4,)), dma((4,)), dma((4,)), dma((2,)), dma((2,)),
            dma((2,)), dma((2,)),
        ] + [dma((8,))] * 8,
        compiler_params=pltpu.CompilerParams(
            collective_id=0, has_side_effects=True, vmem_limit_bytes=LIMIT
        ),
    )(
        schur_x, schur_y, residual_x, residual_y,
        turn(basis_x), turn(basis_y), turn(couple_x), turn(couple_y), coarse_shift,
    )
    return out_x, out_y, turn(values)


def solution(mesh):
    cells = P("sx", "sy", None, None)
    return jax.shard_map(
        shards,
        mesh=mesh,
        in_specs=(cells,) * 8 + (P("sx", "sy", None),),
        out_specs=(cells,) * 3,
        check_vma=False,
    )
```

```python
import functools

import jax
import jax.numpy as jnp
from jax import lax
from jax.experimental import pallas as pl
from jax.experimental.pallas import tpu as pltpu
from jax.sharding import PartitionSpec as P

CITERS = 8
HIGH = lax.Precision.HIGHEST
F = 512
R = 32
PC = 6
B = 128
PANELS = F // B
LIMIT = 56 * 2**20
MESH = pl.DeviceIdType.MESH
CX, CY, SH = 24, 64, 104
SLABS_AFTER, COARSE_AFTER = 0, 1


def dot(a, b, ca=1, cb=0):
    return lax.dot_general(
        a, b, (((ca,), (cb,)), ((), ())), precision=HIGH, preferred_element_type=jnp.float32
    )


def panel_copies(source, target, send, recv, device):
    return [
        pltpu.make_async_remote_copy(
            src_ref=source.at[pl.ds(k * B, B), pl.ds(k * B, F - k * B)],
            dst_ref=target.at[pl.ds(k * B, B), pl.ds(k * B, F - k * B)],
            send_sem=send.at[k],
            recv_sem=recv.at[k],
            device_id=device,
            device_id_type=MESH,
        )
        for k in range(PANELS)
    ]


def flat_row(block, first, stride, width):
    rows, cols = block.shape
    lane = lax.broadcasted_iota(jnp.int32, (cols, width), 1) - first
    hot = jnp.where(
        (lane >= 0) & (lane < stride * rows) & (lane % stride == lax.broadcasted_iota(jnp.int32, (cols, width), 0)),
        1.0,
        0.0,
    )
    spread = dot(block, hot)
    lane = lax.broadcasted_iota(jnp.int32, (rows, width), 1) - first
    own = (lane >= 0) & (lane // stride == lax.broadcasted_iota(jnp.int32, (rows, width), 0))
    return jnp.sum(jnp.where(own, spread, 0.0), axis=0, keepdims=True)


def b_row(b):
    parts = []
    for tile in range(2):
        lane = lax.broadcasted_iota(jnp.int32, (R, B), 1)
        column = 16 * tile + 4 * (lane // 32) + lane % 4
        hot = jnp.where(column == lax.broadcasted_iota(jnp.int32, (R, B), 0), 1.0, 0.0)
        spread = dot(b, hot)
        lane = lax.broadcasted_iota(jnp.int32, (8, B), 1)
        own = (lane % 32) // 4 == lax.broadcasted_iota(jnp.int32, (8, B), 0)
        parts.append(jnp.sum(jnp.where(own, spread, 0.0), axis=0, keepdims=True))
    return parts


def send_round(source_of, target, send, recv, mine, device_of):
    copies = []
    for d in range(1, 8):
        other = lax.rem(mine + d, 8)
        copies.append(
            pltpu.make_async_remote_copy(
                src_ref=source_of(other),
                dst_ref=target.at[mine],
                send_sem=send.at[d],
                recv_sem=recv.at[d],
                device_id=device_of(other),
                device_id_type=MESH,
            )
        )
    for copy in copies:
        copy.start()
    return copies


def rows8(values):
    return jnp.concatenate([values, values], axis=0)


def conjugate_gradients(table, nexts, diag, coarse, remain, search):
    nexts[0:40, :] = pltpu.roll(table[CX : CX + 40, :], F - 1, 1)
    nexts[40:80, :] = pltpu.roll(table[CY : CY + 40, :], F - 32, 1)

    def link(base, a, b):
        return jnp.broadcast_to(table[base + 6 * a + b : base + 6 * a + b + 1, :], (8, F))

    def beyond(base, a, b):
        return jnp.broadcast_to(nexts[base + 6 * a + b : base + 6 * a + b + 1, :], (8, F))

    for k in range(PC):
        total = jnp.broadcast_to(table[SH + k : SH + k + 1, :], (8, F))
        for a in range(PC):
            total += jnp.abs(link(CX, a, k)) + jnp.abs(link(CY, a, k))
            total += jnp.abs(beyond(0, k, a)) + jnp.abs(beyond(40, k, a))
        diag[8 * k : 8 * k + 8, :] = total
        start = rows8(table[4 * k : 4 * k + 4, :])
        coarse[8 * k : 8 * k + 8, :] = jnp.zeros((8, F), jnp.float32)
        remain[8 * k : 8 * k + 8, :] = start
        search[8 * k : 8 * k + 8, :] = start

    def total_of(left, right):
        product = left * right
        part = product[0:8]
        for k in range(1, PC):
            part += product[8 * k : 8 * k + 8]
        part = (part[:, 0:128] + part[:, 128:256]) + (part[:, 256:384] + part[:, 384:512])
        return jnp.broadcast_to(jnp.sum(part, axis=1, keepdims=True), (8, F))

    def sweep(step, now):
        p = search[...]
        low_x, high_x = pltpu.roll(p, 1, 1), pltpu.roll(p, F - 1, 1)
        low_y, high_y = pltpu.roll(p, 32, 1), pltpu.roll(p, F - 32, 1)
        images = []
        for k in range(PC):
            image = diag[8 * k : 8 * k + 8, :] * p[8 * k : 8 * k + 8]
            for a in range(PC):
                rows = slice(8 * a, 8 * a + 8)
                image += link(CX, a, k) * low_x[rows] + beyond(0, k, a) * high_x[rows]
                image += link(CY, a, k) * low_y[rows] + beyond(40, k, a) * high_y[rows]
            images.append(image)
        image = jnp.concatenate(images, axis=0)
        alpha = jnp.concatenate([now / total_of(p, image)] * PC, axis=0)
        coarse[...] += alpha * p
        left = remain[...] - alpha * image
        remain[...] = left
        new = total_of(left, left)
        search[...] = left + jnp.concatenate([new / now] * PC, axis=0) * p
        return new

    first = remain[...]
    lax.fori_loop(0, CITERS, sweep, total_of(first, first))


def spread(values):
    return jnp.broadcast_to(values, (8, B))


def pivots(heads, at, lane, sub):
    heads = list(heads)
    columns = [[spread(head[:, at + c : at + c + 1]) for c in range(8)] for head in heads]
    for c in range(8):
        here = sub == c
        one = jnp.where(here, 1.0, 0.0)
        for f in range(len(heads)):
            own = columns[f][c]
            inverse = 1.0 / spread(own[c : c + 1, :])
            scaled = (own - one) * inverse
            columns[f] = [
                jnp.where(here, inverse, -own * inverse)
                if d == c
                else columns[f][d] - scaled * spread(columns[f][d][c : c + 1, :])
                for d in range(8)
            ]
            heads[f] = heads[f] - scaled * spread(heads[f][c : c + 1, :])
    for f in range(len(heads)):
        for c in range(8):
            heads[f] = jnp.where(lane == at + c, columns[f][c], heads[f])
    return heads


def eliminated(tile, head, at, inside):
    parts = [
        spread(tile[:, at + c : at + c + 1]) * spread(head[c : c + 1, :]) for c in range(8)
    ]
    total = ((parts[0] + parts[1]) + (parts[2] + parts[3])) + (
        (parts[4] + parts[5]) + (parts[6] + parts[7])
    )
    return jnp.where(inside, 0.0, tile) - total


def sixteen(tiles_of, at, lane, sub):
    rests = [jnp.concatenate(tiles[4:], axis=0) for tiles in tiles_of]
    tiles_of = [list(tiles) for tiles in tiles_of]
    for u in range(2):
        first = at + 8 * u
        heads = pivots([tiles[u] for tiles in tiles_of], first, lane, sub)
        inside = (lane >= first) & (lane < first + 8)
        for tiles, head in zip(tiles_of, heads, strict=True):
            tiles[u] = head
            for v in (1 - u, 2, 3):
                tiles[v] = eliminated(tiles[v], head, first, inside)
    inside = (lane >= at) & (lane < at + 16)
    zero = jnp.zeros((8, B), jnp.float32)
    for tiles, rest in zip(tiles_of, rests, strict=True):
        heads = [zero] * (at // 8) + tiles[:2] + [zero] * (B // 8 - 2 - at // 8)
        update = dot(rest, jnp.concatenate(heads, axis=0))
        for t in range(4, B // 8):
            row = (t - 4) * 8
            tiles[t] = jnp.where(inside, 0.0, tiles[t]) - update[row : row + 8, :]
    return tiles_of


def inverses(matrices, unroll=4):
    lane = lax.broadcasted_iota(jnp.int32, (8, B), 1)
    sub = lax.broadcasted_iota(jnp.int32, (8, B), 0)

    def body(step, carry):
        tiles_of = [list(tiles) for tiles in carry]
        for u in range(unroll):
            tiles_of = sixteen(tiles_of, 16 * u, lane, sub)
            tiles_of = [tiles[2:] + tiles[:2] for tiles in tiles_of]
        return tuple(
            tuple(pltpu.roll(tile, B - 16 * unroll, 1) for tile in tiles) for tiles in tiles_of
        )

    start = tuple(tuple(m[8 * t : 8 * t + 8, :] for t in range(B // 8)) for m in matrices)
    end = lax.fori_loop(0, B // 16 // unroll, body, start)
    return [jnp.concatenate(tiles, axis=0) for tiles in end]


def solve_faces(sums, highs, arrivals, sides, weights, between):
    for k in range(PANELS):
        own, rest = slice(k * B, k * B + B), slice(k * B + B, F)
        for a, high, copies in zip(sums, highs, arrivals, strict=True):
            copies[k].wait()
            a[own, k * B :] += high[own, k * B :]
        for a, side, w, inverse in zip(
            sums, sides, weights, inverses([a[own, own] for a in sums]), strict=True
        ):
            part = dot(side[:, own], inverse)
            if k < PANELS - 1:
                row = a[own, rest]
                weight = dot(inverse, row)
                w[own, rest] = weight
                for m in range(k + 1, PANELS):
                    at = (m - k - 1) * B
                    a[m * B : m * B + B, m * B :] -= dot(row[:, at : at + B], weight[:, at:], 0, 0)
                side[:, rest] -= dot(part, row)
            side[:, own] = part
        between(k)
    for k in range(PANELS - 2, -1, -1):
        own, rest = slice(k * B, k * B + B), slice(k * B + B, F)
        for side, w in zip(sides, weights, strict=True):
            side[:, own] -= dot(side[:, rest], w[own, rest], 1, 1)


def lifted(coarse_t, rows):
    total = coarse_t[:, 0:1] * rows[0]
    for k in range(1, PC):
        total += coarse_t[:, k : k + 1] * rows[k]
    return total


def apply(
    schur_x, schur_y, residual_x, residual_y, basis_x, basis_y, couple_x, couple_y, shift,
    out_x, out_y, values,
    high_x, high_y, local_x, local_y, weight_x, weight_y, side_x, side_y, low_x, low_y,
    out_tx, out_ty, in_tx, in_ty,
    msg, near, plane, slabs, whole, table, nexts, diag, coarse, remain, search, back, home,
    load_sem, sx_send, sx_recv, sy_send, sy_recv, t_send, t_recv, u_send, u_recv,
    a_send, a_recv, b_send, b_recv, c_send, c_recv, d_send, d_recv,
):
    i, j = lax.axis_index("sx"), lax.axis_index("sy")
    x_low, x_high = (lax.rem(i + 31, 32), j), (lax.rem(i + 1, 32), j)
    y_low, y_high = (i, lax.rem(j + 15, 16)), (i, lax.rem(j + 1, 16))
    q, y, z = lax.rem(i, 8), lax.rem(j, 2) * 4 + i // 8, j // 2

    def near_of(other):
        return ((i // 8) * 8 + other, j)

    def plane_of(other):
        return (lax.rem(other, 4) * 8 + q, z * 2 + other // 4)

    def stack_of(other):
        return (i, other * 2 + lax.rem(j, 2))

    loads = []
    for s, (source, target) in enumerate(
        ((schur_y.at[0, 0], local_y.at[0]), (schur_x.at[0, 0], local_x.at[0]),
         (schur_x.at[1, 0], local_x.at[1]), (schur_y.at[0, 1], local_y.at[1]))
    ):
        copy = pltpu.make_async_copy(source, target, load_sem.at[s])
        copy.start()
        loads.append(copy)

    barrier = pltpu.get_barrier_semaphore()
    for device in (x_low, x_high, y_low, y_high):
        pl.semaphore_signal(barrier, inc=1, device_id=device, device_id_type=MESH)
    for d in range(1, 8):
        for mine, device_of in ((q, near_of), (y, plane_of), (z, stack_of)):
            pl.semaphore_signal(
                barrier, inc=1, device_id=device_of(lax.rem(mine + d, 8)), device_id_type=MESH
            )
    pl.semaphore_wait(barrier, 25)

    blocks_y = panel_copies(schur_y.at[0, 0], high_y, sy_send, sy_recv, y_low)
    blocks_x = panel_copies(schur_x.at[0, 0], high_x, sx_send, sx_recv, x_low)
    blocks_y[0].start()
    blocks_x[0].start()

    def to_low(source, target, s, device):
        return pltpu.make_async_remote_copy(
            src_ref=source, dst_ref=target, send_sem=t_send.at[s], recv_sem=t_recv.at[s],
            device_id=device, device_id_type=MESH,
        )

    rows_x = [[basis_x[s, k] for k in range(PC)] for s in range(2)]
    rows_y = [[basis_y[0, k, s : s + 1, :] for k in range(PC)] for s in range(2)]
    pad = jnp.zeros((2, F), jnp.float32)
    b = jnp.zeros((8, R), jnp.float32)
    for rows, residual in (
        (rows_x[0], residual_x[0, 0]), (rows_x[1], residual_x[1, 0]),
        (rows_y[0], residual_y[0, 0]), (rows_y[1], residual_y[0, 1]),
    ):
        b += dot(jnp.concatenate(rows + [pad], axis=0), residual, 1, 1)
    b_tiles = b_row(b)
    keep_x, keep_y = (i > 0).astype(jnp.float32), (j > 0).astype(jnp.float32)
    link_x = jnp.concatenate([couple_x[0, a] for a in range(PC)], axis=0) * keep_x
    link_y = jnp.concatenate([couple_y[0, a] for a in range(PC)], axis=0) * keep_y
    links = flat_row(link_x, CX, PC, B) + flat_row(link_y, CY, PC, B) + flat_row(shift[0], SH, PC, B)
    msg[...] = jnp.broadcast_to(jnp.concatenate(b_tiles + [links], axis=1), (8, 3 * B))
    near[q] = msg[...]
    near_copies = send_round(lambda other: msg, near, a_send, a_recv, q, near_of)
    for copy in blocks_x[1:]:
        copy.start()

    loads[0].wait()
    out_ty[...] = dot(residual_y[0, 0], local_y[0])
    t_y = to_low(out_ty, in_ty, 0, y_low)
    t_y.start()
    loads[1].wait()
    out_tx[...] = dot(residual_x[0, 0], local_x[0])
    t_x = to_low(out_tx, in_tx, 1, x_low)
    t_x.start()

    for copy in near_copies:
        copy.wait()
    sub = lax.broadcasted_iota(jnp.int32, (8, 3 * B), 0)
    rows = jnp.zeros((8, 3 * B), jnp.float32)
    for s in range(8):
        rows = jnp.where(sub == s, near[s], rows)
    plane[y] = rows
    plane_copies = send_round(lambda other: plane.at[y], plane, b_send, b_recv, y, plane_of)
    for copy in blocks_y[1:]:
        copy.start()

    loads[2].wait()
    side_x[...] = dot(residual_x[1, 0], local_x[1])
    loads[3].wait()
    side_y[...] = dot(residual_y[0, 1], local_y[1])
    t_x.wait()
    side_x[...] += in_tx[...]
    t_y.wait()
    side_y[...] += in_ty[...]

    stack_copies = []

    home_copies = []

    def coarse_solve():
        for copy in stack_copies:
            copy.wait()
        for s in range(4):
            table[:, s * B : s * B + B] = whole[2 * s : 2 * s + 2].reshape(B, B).T
        conjugate_gradients(table, nexts, diag, coarse, remain, search)

        lane = lax.broadcasted_iota(jnp.int32, (8, B), 1)
        place = y * 8 + q
        for s in range(4):
            first = jnp.zeros((8, B), jnp.float32)
            second = first
            for k in range(PC):
                part = pltpu.roll(coarse[8 * k : 8 * k + 8, s * B : s * B + B], B - place, 1)
                first = jnp.where(lane == k, jnp.broadcast_to(part[:, 0:1], (8, B)), first)
                second = jnp.where(lane == k, jnp.broadcast_to(part[:, 64:65], (8, B)), second)
            back[2 * s] = first
            back[2 * s + 1] = second
        home[z] = back[z]
        home_copies.extend(
            send_round(lambda other: back.at[other], home, d_send, d_recv, z, stack_of)
        )

    def between(k):
        if k == COARSE_AFTER:
            coarse_solve()
        if k != SLABS_AFTER:
            return
        for copy in plane_copies:
            copy.wait()
        lane = lax.broadcasted_iota(jnp.int32, (64, B), 1)
        data = plane[...].reshape(64, 3 * B)
        for s in range(8):
            tile = data[:, B * (s // 4) : B * (s // 4) + B]
            if s % 4:
                tile = pltpu.roll(tile, B - 32 * (s % 4), 1)
            slabs[s] = jnp.where(lane < 24, tile, data[:, 2 * B : 3 * B])
        whole[z] = slabs[z]
        stack_copies.extend(
            send_round(lambda other: slabs.at[other], whole, c_send, c_recv, z, stack_of)
        )

    solve_faces(
        (local_x.at[1], local_y.at[1]), (high_x, high_y), (blocks_x, blocks_y),
        (side_x, side_y), (weight_x, weight_y), between,
    )
    faces = [
        pltpu.make_async_remote_copy(
            src_ref=source, dst_ref=target, send_sem=u_send.at[s], recv_sem=u_recv.at[s],
            device_id=device, device_id_type=MESH,
        )
        for s, (source, target, device) in enumerate(
            ((side_y, low_y, y_high), (side_x, low_x, x_high))
        )
    ]
    for copy in faces:
        copy.start()

    for copy in home_copies:
        copy.wait()
    sub = lax.broadcasted_iota(jnp.int32, (8, B), 0)
    c = jnp.concatenate([jnp.where(sub < 4, home[2 * s], home[2 * s + 1]) for s in range(4)], axis=0)
    turned = jnp.concatenate([c] * 4, axis=0).T
    for k in range(PC):
        values[0, k] = turned[k : k + 1, 0:R]
    out_x[1, 0] = jnp.where(i == 31, residual_x[1, 0], side_x[...]) + lifted(c, rows_x[1])
    out_y[0, 1] = jnp.where(j == 15, residual_y[0, 1], side_y[...]) + lifted(c, rows_y[1])
    faces[1].wait()
    out_x[0, 0] = jnp.where(i == 0, residual_x[0, 0], low_x[...]) + lifted(c, rows_x[0])
    faces[0].wait()
    out_y[0, 0] = jnp.where(j == 0, residual_y[0, 0], low_y[...]) + lifted(c, rows_y[0])


def carry_out(from_x, from_y, from_c, to_x, to_y, to_c, sem):
    copies = [
        pltpu.make_async_copy(source, target, sem.at[s])
        for s, (source, target) in enumerate(((from_x, to_x), (from_y, to_y), (from_c, to_c)))
    ]
    for copy in copies:
        copy.start()
    for copy in copies:
        copy.wait()


def f32(*shape):
    return jax.ShapeDtypeStruct(shape, jnp.float32)


def vmem(*shape):
    return pltpu.VMEM(shape, jnp.float32)


HBM = pl.BlockSpec(memory_space=pl.ANY)
LOCAL = pl.BlockSpec(memory_space=pltpu.VMEM)


def shards(
    schur_x, schur_y, residual_x, residual_y, basis_x, basis_y, couple_x, couple_y, coarse_shift
):
    dma = pltpu.SemaphoreType.DMA

    def turn(array):
        return jnp.swapaxes(array, 1, 2)

    shapes = (f32(2, 1, R, F), f32(1, 2, R, F), f32(1, PC, 1, R))
    results = pl.pallas_call(
        apply,
        name="apply",
        out_shape=shapes,
        in_specs=[HBM] * 2 + [LOCAL] * 7,
        out_specs=(LOCAL,) * 3,
        scratch_shapes=[
            vmem(F, F), vmem(F, F), vmem(2, F, F), vmem(2, F, F), vmem(F, F), vmem(F, F),
        ] + [vmem(R, F)] * 8 + [
            vmem(8, 3 * B), vmem(8, 8, 3 * B), vmem(8, 8, 3 * B), vmem(8, 64, B), vmem(8, 64, B),
            vmem(B, F), vmem(80, F), vmem(8 * PC, F), vmem(8 * PC, F), vmem(8 * PC, F),
            vmem(8 * PC, F), vmem(8, 8, B), vmem(8, 8, B),
            dma((4,)), dma((4,)), dma((4,)), dma((4,)), dma((4,)), dma((2,)), dma((2,)),
            dma((2,)), dma((2,)),
        ] + [dma((8,))] * 8,
        compiler_params=pltpu.CompilerParams(
            collective_id=0, has_side_effects=True, vmem_limit_bytes=LIMIT
        ),
    )(
        schur_x, schur_y, residual_x, residual_y,
        turn(basis_x), turn(basis_y), turn(couple_x), turn(couple_y), coarse_shift,
    )
    out_x, out_y, values = pl.pallas_call(
        carry_out,
        name="carry_out",
        out_shape=shapes,
        in_specs=[HBM] * 3,
        out_specs=(HBM,) * 3,
        scratch_shapes=[dma((3,))],
    )(*results)
    return out_x, out_y, turn(values)


def solution(mesh):
    cells = P("sx", "sy", None, None)
    return jax.shard_map(
        shards,
        mesh=mesh,
        in_specs=(cells,) * 8 + (P("sx", "sy", None),),
        out_specs=(cells,) * 3,
        check_vma=False,
    )
```

```python
import functools

import jax
import jax.numpy as jnp
from jax import lax
from jax.experimental import pallas as pl
from jax.experimental.pallas import tpu as pltpu
from jax.sharding import PartitionSpec as P

CITERS = 8
HIGH = lax.Precision.HIGHEST
F = 512
R = 32
PC = 6
B = 128
PANELS = F // B
LIMIT = 56 * 2**20
MESH = pl.DeviceIdType.MESH
CX, CY, SH = 24, 64, 104
SLABS_AFTER, COARSE_AFTER = 0, 1


def dot(a, b, ca=1, cb=0):
    return lax.dot_general(
        a, b, (((ca,), (cb,)), ((), ())), precision=HIGH, preferred_element_type=jnp.float32
    )


def panel_copies(source, target, send, recv, device):
    copies = []
    for k in range(PANELS):
        for cols in (pl.ds(k * B, B), pl.ds(k * B + B, F - k * B - B)):
            if cols.size:
                part = (pl.ds(k * B, B), cols)
                copies.append(
                    pltpu.make_async_remote_copy(
                        src_ref=source.at[part],
                        dst_ref=target.at[part],
                        send_sem=send.at[len(copies)],
                        recv_sem=recv.at[len(copies)],
                        device_id=device,
                        device_id_type=MESH,
                    )
                )
    return copies


def start_if(flag, copies):
    @pl.when(flag)
    def _():
        for copy in copies:
            copy.start()


def flat_row(block, first, stride, width):
    rows, cols = block.shape
    lane = lax.broadcasted_iota(jnp.int32, (cols, width), 1) - first
    hot = jnp.where(
        (lane >= 0) & (lane < stride * rows) & (lane % stride == lax.broadcasted_iota(jnp.int32, (cols, width), 0)),
        1.0,
        0.0,
    )
    spread = dot(block, hot)
    lane = lax.broadcasted_iota(jnp.int32, (rows, width), 1) - first
    own = (lane >= 0) & (lane // stride == lax.broadcasted_iota(jnp.int32, (rows, width), 0))
    return jnp.sum(jnp.where(own, spread, 0.0), axis=0, keepdims=True)


def b_row(b):
    parts = []
    for tile in range(2):
        lane = lax.broadcasted_iota(jnp.int32, (R, B), 1)
        column = 16 * tile + 4 * (lane // 32) + lane % 4
        hot = jnp.where(column == lax.broadcasted_iota(jnp.int32, (R, B), 0), 1.0, 0.0)
        spread = dot(b, hot)
        lane = lax.broadcasted_iota(jnp.int32, (8, B), 1)
        own = (lane % 32) // 4 == lax.broadcasted_iota(jnp.int32, (8, B), 0)
        parts.append(jnp.sum(jnp.where(own, spread, 0.0), axis=0, keepdims=True))
    return parts


def send_round(source_of, target, send, recv, mine, device_of):
    copies = []
    for d in range(1, 8):
        other = lax.rem(mine + d, 8)
        copies.append(
            pltpu.make_async_remote_copy(
                src_ref=source_of(other),
                dst_ref=target.at[mine],
                send_sem=send.at[d],
                recv_sem=recv.at[d],
                device_id=device_of(other),
                device_id_type=MESH,
            )
        )
    for copy in copies:
        copy.start()
    return copies


def rows8(values):
    return jnp.concatenate([values, values], axis=0)


def conjugate_gradients(table, nexts, diag, coarse, remain, search):
    nexts[0:40, :] = pltpu.roll(table[CX : CX + 40, :], F - 1, 1)
    nexts[40:80, :] = pltpu.roll(table[CY : CY + 40, :], F - 32, 1)

    def link(base, a, b):
        return jnp.broadcast_to(table[base + 6 * a + b : base + 6 * a + b + 1, :], (8, F))

    def beyond(base, a, b):
        return jnp.broadcast_to(nexts[base + 6 * a + b : base + 6 * a + b + 1, :], (8, F))

    for k in range(PC):
        total = jnp.broadcast_to(table[SH + k : SH + k + 1, :], (8, F))
        for a in range(PC):
            total += jnp.abs(link(CX, a, k)) + jnp.abs(link(CY, a, k))
            total += jnp.abs(beyond(0, k, a)) + jnp.abs(beyond(40, k, a))
        diag[8 * k : 8 * k + 8, :] = total
        start = rows8(table[4 * k : 4 * k + 4, :])
        coarse[8 * k : 8 * k + 8, :] = jnp.zeros((8, F), jnp.float32)
        remain[8 * k : 8 * k + 8, :] = start
        search[8 * k : 8 * k + 8, :] = start

    def total_of(left, right):
        product = left * right
        part = product[0:8]
        for k in range(1, PC):
            part += product[8 * k : 8 * k + 8]
        part = (part[:, 0:128] + part[:, 128:256]) + (part[:, 256:384] + part[:, 384:512])
        return jnp.broadcast_to(jnp.sum(part, axis=1, keepdims=True), (8, F))

    def sweep(step, now):
        p = search[...]
        low_x, high_x = pltpu.roll(p, 1, 1), pltpu.roll(p, F - 1, 1)
        low_y, high_y = pltpu.roll(p, 32, 1), pltpu.roll(p, F - 32, 1)
        images = []
        for k in range(PC):
            image = diag[8 * k : 8 * k + 8, :] * p[8 * k : 8 * k + 8]
            for a in range(PC):
                rows = slice(8 * a, 8 * a + 8)
                image += link(CX, a, k) * low_x[rows] + beyond(0, k, a) * high_x[rows]
                image += link(CY, a, k) * low_y[rows] + beyond(40, k, a) * high_y[rows]
            images.append(image)
        image = jnp.concatenate(images, axis=0)
        alpha = jnp.concatenate([now / total_of(p, image)] * PC, axis=0)
        coarse[...] += alpha * p
        left = remain[...] - alpha * image
        remain[...] = left
        new = total_of(left, left)
        search[...] = left + jnp.concatenate([new / now] * PC, axis=0) * p
        return new

    first = remain[...]
    lax.fori_loop(0, CITERS, sweep, total_of(first, first))


def spread(values):
    return jnp.broadcast_to(values, (8, B))


def pivots(heads, at, lane, sub):
    heads = list(heads)
    columns = [[spread(head[:, at + c : at + c + 1]) for c in range(8)] for head in heads]
    for c in range(8):
        here = sub == c
        one = jnp.where(here, 1.0, 0.0)
        for f in range(len(heads)):
            own = columns[f][c]
            inverse = 1.0 / spread(own[c : c + 1, :])
            scaled = (own - one) * inverse
            columns[f] = [
                jnp.where(here, inverse, -own * inverse)
                if d == c
                else columns[f][d] - scaled * spread(columns[f][d][c : c + 1, :])
                for d in range(8)
            ]
            heads[f] = heads[f] - scaled * spread(heads[f][c : c + 1, :])
    for f in range(len(heads)):
        for c in range(8):
            heads[f] = jnp.where(lane == at + c, columns[f][c], heads[f])
    return heads


def eliminated(tile, head, at, inside):
    parts = [
        spread(tile[:, at + c : at + c + 1]) * spread(head[c : c + 1, :]) for c in range(8)
    ]
    total = ((parts[0] + parts[1]) + (parts[2] + parts[3])) + (
        (parts[4] + parts[5]) + (parts[6] + parts[7])
    )
    return jnp.where(inside, 0.0, tile) - total


def sixteen(tiles_of, at, lane, sub):
    rests = [jnp.concatenate(tiles[4:], axis=0) for tiles in tiles_of]
    tiles_of = [list(tiles) for tiles in tiles_of]
    for u in range(2):
        first = at + 8 * u
        heads = pivots([tiles[u] for tiles in tiles_of], first, lane, sub)
        inside = (lane >= first) & (lane < first + 8)
        for tiles, head in zip(tiles_of, heads, strict=True):
            tiles[u] = head
            for v in (1 - u, 2, 3):
                tiles[v] = eliminated(tiles[v], head, first, inside)
    inside = (lane >= at) & (lane < at + 16)
    zero = jnp.zeros((8, B), jnp.float32)
    for tiles, rest in zip(tiles_of, rests, strict=True):
        heads = [zero] * (at // 8) + tiles[:2] + [zero] * (B // 8 - 2 - at // 8)
        update = dot(rest, jnp.concatenate(heads, axis=0))
        for t in range(4, B // 8):
            row = (t - 4) * 8
            tiles[t] = jnp.where(inside, 0.0, tiles[t]) - update[row : row + 8, :]
    return tiles_of


def inverses(matrices, unroll=4):
    lane = lax.broadcasted_iota(jnp.int32, (8, B), 1)
    sub = lax.broadcasted_iota(jnp.int32, (8, B), 0)

    def body(step, carry):
        tiles_of = [list(tiles) for tiles in carry]
        for u in range(unroll):
            tiles_of = sixteen(tiles_of, 16 * u, lane, sub)
            tiles_of = [tiles[2:] + tiles[:2] for tiles in tiles_of]
        return tuple(
            tuple(pltpu.roll(tile, B - 16 * unroll, 1) for tile in tiles) for tiles in tiles_of
        )

    start = tuple(tuple(m[8 * t : 8 * t + 8, :] for t in range(B // 8)) for m in matrices)
    end = lax.fori_loop(0, B // 16 // unroll, body, start)
    return [jnp.concatenate(tiles, axis=0) for tiles in end]


def solve_faces(sums, highs, arrived, sides, weights, between):
    for k in range(PANELS):
        own, rest = slice(k * B, k * B + B), slice(k * B + B, F)
        arrived(2 * k)
        for a, high in zip(sums, highs, strict=True):
            a[own, own] += high[own, own]
        inverted = inverses([a[own, own] for a in sums])
        if k < PANELS - 1:
            arrived(2 * k + 1)
            for a, high in zip(sums, highs, strict=True):
                a[own, rest] += high[own, rest]
        for a, side, w, inverse in zip(sums, sides, weights, inverted, strict=True):
            part = dot(side[:, own], inverse)
            if k < PANELS - 1:
                row = a[own, rest]
                weight = dot(inverse, row)
                w[own, rest] = weight
                for m in range(k + 1, PANELS):
                    at = (m - k - 1) * B
                    a[m * B : m * B + B, m * B :] -= dot(row[:, at : at + B], weight[:, at:], 0, 0)
                side[:, rest] -= dot(part, row)
            side[:, own] = part
        between(k)
    for k in range(PANELS - 2, -1, -1):
        own, rest = slice(k * B, k * B + B), slice(k * B + B, F)
        for side, w in zip(sides, weights, strict=True):
            side[:, own] -= dot(side[:, rest], w[own, rest], 1, 1)


def lifted(coarse_t, rows):
    total = coarse_t[:, 0:1] * rows[0]
    for k in range(1, PC):
        total += coarse_t[:, k : k + 1] * rows[k]
    return total


def apply(
    schur_x, schur_y, residual_x, residual_y, basis_x, basis_y, couple_x, couple_y, shift,
    out_x, out_y, values,
    high_x, high_y, local_x, local_y, weight_x, weight_y, side_x, side_y, low_x, low_y,
    out_tx, out_ty, in_tx, in_ty,
    msg, near, plane, slabs, whole, table, nexts, diag, coarse, remain, search, back, home,
    load_sem, sx_send, sx_recv, sy_send, sy_recv, t_send, t_recv, u_send, u_recv,
    a_send, a_recv, b_send, b_recv, c_send, c_recv, d_send, d_recv,
):
    i, j = lax.axis_index("sx"), lax.axis_index("sy")
    x_low, x_high = (lax.rem(i + 31, 32), j), (lax.rem(i + 1, 32), j)
    y_low, y_high = (i, lax.rem(j + 15, 16)), (i, lax.rem(j + 1, 16))
    q, y, z = lax.rem(i, 8), lax.rem(j, 2) * 4 + i // 8, j // 2

    def near_of(other):
        return ((i // 8) * 8 + other, j)

    def plane_of(other):
        return (lax.rem(other, 4) * 8 + q, z * 2 + other // 4)

    def stack_of(other):
        return (i, other * 2 + lax.rem(j, 2))

    loads = []
    for s, (source, target) in enumerate(
        ((schur_y.at[0, 0], local_y.at[0]), (schur_x.at[0, 0], local_x.at[0]),
         (schur_x.at[1, 0], local_x.at[1]), (schur_y.at[0, 1], local_y.at[1]))
    ):
        copy = pltpu.make_async_copy(source, target, load_sem.at[s])
        copy.start()
        loads.append(copy)

    barrier = pltpu.get_barrier_semaphore()
    for device in (x_low, x_high, y_low, y_high):
        pl.semaphore_signal(barrier, inc=1, device_id=device, device_id_type=MESH)
    for d in range(1, 8):
        for mine, device_of in ((q, near_of), (y, plane_of), (z, stack_of)):
            pl.semaphore_signal(
                barrier, inc=1, device_id=device_of(lax.rem(mine + d, 8)), device_id_type=MESH
            )
    pl.semaphore_wait(barrier, 25)

    blocks_y = panel_copies(schur_y.at[0, 0], high_y, sy_send, sy_recv, y_low)
    blocks_x = panel_copies(schur_x.at[0, 0], high_x, sx_send, sx_recv, x_low)
    send_x, send_y, take_x, take_y = i > 0, j > 0, i < 31, j < 15
    start_if(send_y, blocks_y[:3])
    start_if(send_x, blocks_x[:3])

    @pl.when(i == 31)
    def _():
        high_x[...] = jnp.zeros((F, F), jnp.float32)

    @pl.when(j == 15)
    def _():
        high_y[...] = jnp.zeros((F, F), jnp.float32)

    def arrived(index):
        @pl.when(take_x)
        def _():
            blocks_x[index].wait_recv()

        @pl.when(take_y)
        def _():
            blocks_y[index].wait_recv()

    def to_low(source, target, s, device):
        return pltpu.make_async_remote_copy(
            src_ref=source, dst_ref=target, send_sem=t_send.at[s], recv_sem=t_recv.at[s],
            device_id=device, device_id_type=MESH,
        )

    rows_x = [[basis_x[s, k] for k in range(PC)] for s in range(2)]
    rows_y = [[basis_y[0, k, s : s + 1, :] for k in range(PC)] for s in range(2)]
    pad = jnp.zeros((2, F), jnp.float32)
    b = jnp.zeros((8, R), jnp.float32)
    for rows, residual in (
        (rows_x[0], residual_x[0, 0]), (rows_x[1], residual_x[1, 0]),
        (rows_y[0], residual_y[0, 0]), (rows_y[1], residual_y[0, 1]),
    ):
        b += dot(jnp.concatenate(rows + [pad], axis=0), residual, 1, 1)
    b_tiles = b_row(b)
    keep_x, keep_y = (i > 0).astype(jnp.float32), (j > 0).astype(jnp.float32)
    link_x = jnp.concatenate([couple_x[0, a] for a in range(PC)], axis=0) * keep_x
    link_y = jnp.concatenate([couple_y[0, a] for a in range(PC)], axis=0) * keep_y
    links = flat_row(link_x, CX, PC, B) + flat_row(link_y, CY, PC, B) + flat_row(shift[0], SH, PC, B)
    msg[...] = jnp.broadcast_to(jnp.concatenate(b_tiles + [links], axis=1), (8, 3 * B))
    near[q] = msg[...]
    near_copies = send_round(lambda other: msg, near, a_send, a_recv, q, near_of)
    start_if(send_x, blocks_x[3:])

    loads[0].wait()
    out_ty[...] = dot(residual_y[0, 0], local_y[0])
    t_y = to_low(out_ty, in_ty, 0, y_low)
    t_y.start()
    loads[1].wait()
    out_tx[...] = dot(residual_x[0, 0], local_x[0])
    t_x = to_low(out_tx, in_tx, 1, x_low)
    t_x.start()

    for copy in near_copies:
        copy.wait()
    sub = lax.broadcasted_iota(jnp.int32, (8, 3 * B), 0)
    rows = jnp.zeros((8, 3 * B), jnp.float32)
    for s in range(8):
        rows = jnp.where(sub == s, near[s], rows)
    plane[y] = rows
    plane_copies = send_round(lambda other: plane.at[y], plane, b_send, b_recv, y, plane_of)
    start_if(send_y, blocks_y[3:])

    loads[2].wait()
    side_x[...] = dot(residual_x[1, 0], local_x[1])
    loads[3].wait()
    side_y[...] = dot(residual_y[0, 1], local_y[1])
    t_x.wait()
    side_x[...] += in_tx[...]
    t_y.wait()
    side_y[...] += in_ty[...]

    stack_copies = []

    home_copies = []

    def coarse_solve():
        for copy in stack_copies:
            copy.wait()
        for s in range(4):
            table[:, s * B : s * B + B] = whole[2 * s : 2 * s + 2].reshape(B, B).T
        conjugate_gradients(table, nexts, diag, coarse, remain, search)

        lane = lax.broadcasted_iota(jnp.int32, (8, B), 1)
        place = y * 8 + q
        for s in range(4):
            first = jnp.zeros((8, B), jnp.float32)
            second = first
            for k in range(PC):
                part = pltpu.roll(coarse[8 * k : 8 * k + 8, s * B : s * B + B], B - place, 1)
                first = jnp.where(lane == k, jnp.broadcast_to(part[:, 0:1], (8, B)), first)
                second = jnp.where(lane == k, jnp.broadcast_to(part[:, 64:65], (8, B)), second)
            back[2 * s] = first
            back[2 * s + 1] = second
        home[z] = back[z]
        home_copies.extend(
            send_round(lambda other: back.at[other], home, d_send, d_recv, z, stack_of)
        )

    def between(k):
        if k == COARSE_AFTER:
            coarse_solve()
        if k != SLABS_AFTER:
            return
        for copy in plane_copies:
            copy.wait()
        lane = lax.broadcasted_iota(jnp.int32, (64, B), 1)
        data = plane[...].reshape(64, 3 * B)
        for s in range(8):
            tile = data[:, B * (s // 4) : B * (s // 4) + B]
            if s % 4:
                tile = pltpu.roll(tile, B - 32 * (s % 4), 1)
            slabs[s] = jnp.where(lane < 24, tile, data[:, 2 * B : 3 * B])
        whole[z] = slabs[z]
        stack_copies.extend(
            send_round(lambda other: slabs.at[other], whole, c_send, c_recv, z, stack_of)
        )

    solve_faces(
        (local_x.at[1], local_y.at[1]), (high_x, high_y), arrived,
        (side_x, side_y), (weight_x, weight_y), between,
    )
    faces = [
        pltpu.make_async_remote_copy(
            src_ref=source, dst_ref=target, send_sem=u_send.at[s], recv_sem=u_recv.at[s],
            device_id=device, device_id_type=MESH,
        )
        for s, (source, target, device) in enumerate(
            ((side_y, low_y, y_high), (side_x, low_x, x_high))
        )
    ]
    for copy in faces:
        copy.start()

    for copy in home_copies:
        copy.wait()
    sub = lax.broadcasted_iota(jnp.int32, (8, B), 0)
    c = jnp.concatenate([jnp.where(sub < 4, home[2 * s], home[2 * s + 1]) for s in range(4)], axis=0)
    turned = jnp.concatenate([c] * 4, axis=0).T
    for k in range(PC):
        values[0, k] = turned[k : k + 1, 0:R]
    out_x[1, 0] = jnp.where(i == 31, residual_x[1, 0], side_x[...]) + lifted(c, rows_x[1])
    out_y[0, 1] = jnp.where(j == 15, residual_y[0, 1], side_y[...]) + lifted(c, rows_y[1])
    faces[1].wait()
    out_x[0, 0] = jnp.where(i == 0, residual_x[0, 0], low_x[...]) + lifted(c, rows_x[0])
    for flag, blocks in ((send_x, blocks_x), (send_y, blocks_y)):

        @pl.when(flag)
        def _(blocks=blocks):
            for copy in blocks:
                copy.wait_send()

    faces[0].wait()
    out_y[0, 0] = jnp.where(j == 0, residual_y[0, 0], low_y[...]) + lifted(c, rows_y[0])


def carry_out(from_x, from_y, from_c, to_x, to_y, to_c):
    to_x[...] = from_x[...]
    to_y[...] = from_y[...]
    to_c[...] = from_c[...]


def f32(*shape):
    return jax.ShapeDtypeStruct(shape, jnp.float32)


def vmem(*shape):
    return pltpu.VMEM(shape, jnp.float32)


HBM = pl.BlockSpec(memory_space=pl.ANY)
LOCAL = pl.BlockSpec(memory_space=pltpu.VMEM)


def shards(
    schur_x, schur_y, residual_x, residual_y, basis_x, basis_y, couple_x, couple_y, coarse_shift
):
    dma = pltpu.SemaphoreType.DMA

    def turn(array):
        return jnp.swapaxes(array, 1, 2)

    shapes = (f32(2, 1, R, F), f32(1, 2, R, F), f32(1, PC, 1, R))
    results = pl.pallas_call(
        apply,
        name="apply",
        out_shape=shapes,
        in_specs=[HBM] * 2 + [LOCAL] * 7,
        out_specs=(LOCAL,) * 3,
        scratch_shapes=[
            vmem(F, F), vmem(F, F), vmem(2, F, F), vmem(2, F, F), vmem(F, F), vmem(F, F),
        ] + [vmem(R, F)] * 8 + [
            vmem(8, 3 * B), vmem(8, 8, 3 * B), vmem(8, 8, 3 * B), vmem(8, 64, B), vmem(8, 64, B),
            vmem(B, F), vmem(80, F), vmem(8 * PC, F), vmem(8 * PC, F), vmem(8 * PC, F),
            vmem(8 * PC, F), vmem(8, 8, B), vmem(8, 8, B),
            dma((4,)), dma((7,)), dma((7,)), dma((7,)), dma((7,)), dma((2,)), dma((2,)),
            dma((2,)), dma((2,)),
        ] + [dma((8,))] * 8,
        compiler_params=pltpu.CompilerParams(
            collective_id=0, has_side_effects=True, vmem_limit_bytes=LIMIT
        ),
    )(
        schur_x, schur_y, residual_x, residual_y,
        turn(basis_x), turn(basis_y), turn(couple_x), turn(couple_y), coarse_shift,
    )
    out_x, out_y, values = pl.pallas_call(
        carry_out,
        name="carry_out",
        out_shape=shapes,
        in_specs=[LOCAL] * 3,
        out_specs=(LOCAL,) * 3,
    )(*results)
    return out_x, out_y, turn(values)


def solution(mesh):
    cells = P("sx", "sy", None, None)
    return jax.shard_map(
        shards,
        mesh=mesh,
        in_specs=(cells,) * 8 + (P("sx", "sy", None),),
        out_specs=(cells,) * 3,
        check_vma=False,
    )
```
